32 devices in a mesh: dp: 4 (over y, core), proto: 8 (over z, x).
Axes of the slice: x: 2, y: 2, z: 4, core: 2. Of those that a mesh axis runs over, the one named last changes fastest.
Arguments:
- student_cls: bfloat16 [32, 1536], P(('dp', 'proto')), may hold values from -6 to 6
- student_patches: bfloat16 [32, 256, 1536], P(('dp', 'proto')), may hold values from -6 to 6
- teacher_cls: bfloat16 [32, 1536], P(('dp', 'proto')), may hold values from -6 to 6
- teacher_patches: bfloat16 [32, 256, 1536], P(('dp', 'proto')), may hold values from -6 to 6
- mask_index: int32 [32, 31], P(('dp', 'proto')), may hold values from 0 to 255, as said below
- crop_pair: int32 [32], P(('dp', 'proto')), may hold values from 0 to 7, as said below
- center: float32 [2, 65536], P(None, 'proto'), may hold values from -0.3 to 0.3
- student_w1: bfloat16 [1536, 2048], P('dp', 'proto'), may hold values from -0.15625 to 0.15625
- student_w2: bfloat16 [2048, 256], P('proto'), may hold values from -0.06970923 to 0.06970923
- teacher_w1: bfloat16 [1536, 2048], P('dp', 'proto'), may hold values from -0.15625 to 0.15625
- teacher_w2: bfloat16 [2048, 256], P('proto'), may hold values from -0.06970923 to 0.06970923
- student_proto: float32 [256, 65536], P(None, 'proto'), may hold values from -0.39 to 0.39
- teacher_proto: float32 [256, 65536], P(None, 'proto'), may hold values from -0.39 to 0.39
Outputs:
- loss_value: float32 [4], P('dp')
- grad_w1: float32 [1536, 2048], P('dp', 'proto')
- grad_w2: float32 [2048, 256], P('proto')
- grad_proto: float32 [256, 65536], P('dp', 'proto')
The draws below stay inside these ranges and needn't reach their ends.
Inputs may be any that keep to these rules, and one draw needn't show every extreme that they name: `mask_index`: the 31 indices of one crop are distinct. Within each dp index's 8 crops, crop_pair pairs crops: crop_pair[crop_pair[c]] = c and crop_pair[c] != c.
All inputs are finite; a program needn't handle non-finite values.
Results may differ from the reference program's by a relative error of at most 0.006.
Values may be sent and summed in bfloat16 or wider, within the bound.
A program may use at most 128 MiB of HBM per device.

```python
import jax
import jax.numpy as jnp
from jax import lax

D = 1536
HID = 2048
BOT = 256
PROTOS = 65536
PATCH = 256
MASKED = 31
CROP_GROUP = 8
CROPS = 32
N_DP = 4


def shared_pattern(key):
    direction = jax.random.truncated_normal(jax.random.fold_in(key, 101), -3.0, 3.0, (BOT,), jnp.float32)
    roughness = jax.random.truncated_normal(jax.random.fold_in(key, 102), -3.0, 3.0, (PROTOS,), jnp.float32)
    return (direction, roughness)


def unit_jitter(key, extent):
    normal_part = jax.random.truncated_normal(jax.random.fold_in(key, 1), -3.0, 3.0, extent, jnp.float32)
    return normal_part


def bottleneck_layer(key, direction, lift_gain):
    jitter = unit_jitter(key, (HID, BOT))
    return (jitter * HID ** (-0.5) + lift_gain / HID * direction[None, :]).astype(jnp.bfloat16)


def prototype_layer(key, direction, roughness, tilt, spread):
    jitter = unit_jitter(key, (BOT, PROTOS))
    position = jnp.arange(PROTOS, dtype=jnp.float32) * (2.0 / (PROTOS - 1)) - 1.0
    alignment = tilt * position + spread * roughness
    return 0.05 * (jitter + direction[:, None] * alignment[None, :])


def draw_mask_index(key, part):
    key = jax.random.fold_in(key, 11)
    crop_keys = jax.random.split(key, CROPS)

    def draw_single(sub_key):
        return jax.random.permutation(sub_key, PATCH)[:MASKED].astype(jnp.int32)
    return jax.vmap(draw_single)(crop_keys)


def draw_crop_pair(key, part):
    key = jax.random.fold_in(key, 23)
    group_keys = jax.random.split(key, N_DP)

    def draw_single(sub_key):
        shuffled = jax.random.permutation(sub_key, CROP_GROUP).astype(jnp.int32)
        partner_of = shuffled[jnp.arange(CROP_GROUP, dtype=jnp.int32) ^ 1]
        return jnp.zeros((CROP_GROUP,), jnp.int32).at[shuffled].set(partner_of)
    return jax.vmap(draw_single)(group_keys).reshape(CROPS)


def draw_student_w2(key, part):
    direction, _ = shared_pattern(key)
    key = jax.random.fold_in(key, 31)
    return bottleneck_layer(key, direction, 2.28)


def draw_teacher_w2(key, part):
    direction, _ = shared_pattern(key)
    key = jax.random.fold_in(key, 37)
    return bottleneck_layer(key, direction, 2.28)


def draw_student_proto(key, part):
    direction, roughness = shared_pattern(key)
    key = jax.random.fold_in(key, 41)
    return prototype_layer(key, direction, roughness, 0.23, 0.45)


def draw_teacher_proto(key, part):
    direction, roughness = shared_pattern(key)
    key = jax.random.fold_in(key, 43)
    return prototype_layer(key, direction, roughness, 0.23, 0.45)


def block_levels(key, shape, pieces, low, high):
    factor_of = 1.0
    for dim, shards_of in pieces:
        heights = jax.random.uniform(jax.random.fold_in(jax.random.fold_in(key, 6), dim), (shards_of,), jnp.float32, low / len(pieces), high / len(pieces))
        factor_of = factor_of * jnp.repeat(jnp.exp(heights), shape[dim] // shards_of).reshape((-1,) + (1,) * (len(shape) - 1 - dim))
    return factor_of


def noise(rng, shape, width, limit, pieces=(), held_as=jnp.bfloat16):
    gain = block_levels(rng, shape, pieces, -0.22, 0.18) if pieces else 1.0
    array = jax.random.normal(rng, shape, jnp.float32) * width * gain
    return jnp.minimum(jnp.maximum(array, -limit), limit).astype(held_as)


def setup_inputs(seed: int = 0) -> dict:
    streams_of = jax.random.split(jax.random.key(seed), 14)
    student_cls = noise(streams_of[0], (CROPS, D), 1.0, 6.0, ((0, 32),))
    student_patches = noise(streams_of[1], (CROPS, PATCH, D), 1.0, 6.0, ((0, 32),))
    teacher_cls = noise(streams_of[2], (CROPS, D), 1.0, 6.0, ((0, 32),))
    teacher_patches = noise(streams_of[3], (CROPS, PATCH, D), 1.0, 6.0, ((0, 32),))
    mask_index = draw_mask_index(jax.random.fold_in(streams_of[13], 71), 0)
    crop_pair = draw_crop_pair(jax.random.fold_in(streams_of[13], 71), 0)
    center = jnp.clip(jax.random.uniform(streams_of[6], (2, PROTOS), jnp.float32, -0.3, 0.3) * block_levels(streams_of[6], (2, PROTOS), ((1, 8),), -0.4, 0.0), -0.3, 0.3)
    student_w1 = noise(streams_of[7], (D, HID), D ** -0.5, 0.15625, ((0, 4), (1, 8)))
    student_w2 = draw_student_w2(jax.random.fold_in(streams_of[13], 71), 0)
    teacher_w1 = noise(streams_of[9], (D, HID), D ** -0.5, 0.15625, ((0, 4), (1, 8)))
    teacher_w2 = draw_teacher_w2(jax.random.fold_in(streams_of[13], 71), 0)
    student_proto = draw_student_proto(jax.random.fold_in(streams_of[13], 71), 0)
    teacher_proto = draw_teacher_proto(jax.random.fold_in(streams_of[13], 71), 0)
    return {"student_cls": student_cls, "student_patches": student_patches, "teacher_cls": teacher_cls, "teacher_patches": teacher_patches, "mask_index": mask_index, "crop_pair": crop_pair, "center": center, "student_w1": student_w1, "student_w2": student_w2, "teacher_w1": teacher_w1, "teacher_w2": teacher_w2, "student_proto": student_proto, "teacher_proto": teacher_proto}


epsilon = 1e-06
teacher_temp = 0.07
student_temp = 0.1
loss_scale = 1048576.0

def select_rows(cls_tokens, patches, mask_index):
    picked = jax.vmap(lambda patch_set, index_set: patch_set[index_set])(patches, mask_index)
    joined = jnp.concatenate([cls_tokens[:, None, :], picked], axis=1)
    return joined.reshape(-1, cls_tokens.shape[-1])

def head_forward(rows, first, second):
    preact = jnp.dot(rows, first, preferred_element_type=jnp.float32)
    hidden = jax.nn.gelu(preact, approximate=False).astype(jnp.bfloat16)
    bottle = jnp.dot(hidden, second, preferred_element_type=jnp.float32)
    inverse = lax.rsqrt(lax.optimization_barrier(jnp.sum(bottle * bottle, axis=-1, keepdims=True)) + epsilon)
    return (preact, hidden, bottle * inverse, inverse)

def normalize_columns(proto):
    inverse = lax.rsqrt(lax.optimization_barrier(jnp.sum(proto * proto, axis=0, keepdims=True)) + epsilon)
    return (proto * inverse, inverse)

def gelu_grad(preact):
    normal_cdf = 0.5 * (1.0 + lax.erf(preact * 0.7071067811865476))
    normal_pdf = jnp.exp(-0.5 * preact * preact) * 0.3989422804014327
    return normal_cdf + preact * normal_pdf

def reference(student_cls, student_patches, teacher_cls, teacher_patches, mask_index, crop_pair, center, student_w1, student_w2, teacher_w1, teacher_w2, student_proto, teacher_proto):
    row_span = MASKED + 1
    group_rows = CROP_GROUP * row_span
    rows_student = select_rows(student_cls, student_patches, mask_index)
    rows_teacher = select_rows(teacher_cls, teacher_patches, mask_index)
    preact, hidden, unit_s, inverse_s = head_forward(rows_student, student_w1, student_w2)
    _, _, unit_t, _ = head_forward(rows_teacher, teacher_w1, teacher_w2)
    proto_unit, col_inverse = normalize_columns(student_proto)
    teacher_unit, _ = normalize_columns(teacher_proto)
    proto_s_b = proto_unit.astype(jnp.bfloat16)
    proto_t_b = teacher_unit.astype(jnp.bfloat16)
    index_rows = jnp.arange(group_rows, dtype=jnp.int32)
    is_cls = index_rows % row_span == 0
    crop_local = (index_rows // row_span).astype(jnp.int32)
    weights = jnp.where(is_cls, 1.0 / CROPS, 1.0 / (CROPS * MASKED)).astype(jnp.float32)
    units_s = unit_s.astype(jnp.bfloat16).reshape(N_DP, group_rows, BOT)
    units_t = unit_t.astype(jnp.bfloat16).reshape(N_DP, group_rows, BOT)
    pair_groups = crop_pair.reshape(N_DP, CROP_GROUP)
    shift = jnp.where(is_cls[:, None], center[0][None, :], center[1][None, :])

    def per_group(grad_sum, inputs):
        group_s, group_t, group_pairs = inputs
        target = jnp.where(is_cls, group_pairs[crop_local] * row_span, index_rows).astype(jnp.int32)
        aligned = group_t[target]
        logit_s = jnp.dot(group_s, proto_s_b, preferred_element_type=jnp.float32) / student_temp
        logit_t = (jnp.dot(aligned, proto_t_b, preferred_element_type=jnp.float32) - shift) / teacher_temp
        exp_teacher = jnp.exp(logit_t)
        exp_student = jnp.exp(logit_s)
        total_t = lax.optimization_barrier(jnp.sum(exp_teacher, axis=1))
        total_s = lax.optimization_barrier(jnp.sum(exp_student, axis=1))
        cross_term = lax.optimization_barrier(jnp.sum(exp_teacher * logit_s, axis=1)) / total_t
        row_loss = jnp.log(total_s) - cross_term
        loss_part = jnp.sum(weights * row_loss) * N_DP
        factor = loss_scale / student_temp * weights
        dscore = (factor[:, None] * (exp_student / total_s[:, None] - exp_teacher / total_t[:, None])).astype(jnp.bfloat16)
        grad_unit = lax.dot_general(dscore, proto_s_b, (((1,), (1,)), ((), ())), preferred_element_type=jnp.float32)
        grad_part = lax.dot_general(group_s, dscore, (((0,), (0,)), ((), ())), preferred_element_type=jnp.float32)
        return (grad_sum + grad_part, (grad_unit, loss_part))
    initial = jnp.zeros((BOT, PROTOS), jnp.float32)
    grad_cols, (grad_units, loss_value) = lax.scan(per_group, initial, (units_s, units_t, pair_groups))
    grad_units = grad_units.reshape(-1, BOT)
    grad_proto = col_inverse * (grad_cols - proto_unit * lax.optimization_barrier(jnp.sum(proto_unit * grad_cols, axis=0, keepdims=True)))
    grad_z = (inverse_s * (grad_units - unit_s * lax.optimization_barrier(jnp.sum(unit_s * grad_units, axis=1, keepdims=True)))).astype(jnp.bfloat16)
    grad_hidden = lax.dot_general(grad_z, student_w2, (((1,), (1,)), ((), ())), preferred_element_type=jnp.float32)
    grad_pre = (grad_hidden * gelu_grad(preact)).astype(jnp.bfloat16)
    grad_w2 = lax.dot_general(hidden, grad_z, (((0,), (0,)), ((), ())), preferred_element_type=jnp.float32)
    grad_w1 = lax.dot_general(rows_student, grad_pre, (((0,), (0,)), ((), ())), preferred_element_type=jnp.float32)
    return (loss_value, grad_w1, grad_w2, grad_proto)
```

```python
import functools
import math

import jax
import jax.numpy as jnp
from jax import lax
from jax.experimental import pallas as pl
from jax.experimental.pallas import tpu as pltpu
from jax.sharding import PartitionSpec as P

epsilon = 1e-06
teacher_temp = 0.07
student_temp = 0.1
loss_scale = 1048576.0


def select_rows(cls_tokens, patches, mask_index):
    picked = jax.vmap(lambda patch_set, index_set: patch_set[index_set])(patches, mask_index)
    joined = jnp.concatenate([cls_tokens[:, None, :], picked], axis=1)
    return joined.reshape(-1, cls_tokens.shape[-1])


def normalize_rows(bottle):
    inverse = lax.rsqrt(jnp.sum(bottle * bottle, axis=-1, keepdims=True) + epsilon)
    return (bottle * inverse, inverse)


def normalize_columns(proto):
    inverse = lax.rsqrt(jnp.sum(proto * proto, axis=0, keepdims=True) + epsilon)
    return (proto * inverse, inverse)


def gelu_grad(preact):
    normal_cdf = 0.5 * (1.0 + lax.erf(preact * 0.7071067811865476))
    normal_pdf = jnp.exp(-0.5 * preact * preact) * 0.3989422804014327
    return normal_cdf + preact * normal_pdf


def contract_rows(left, right):
    return lax.dot_general(
        left, right, (((0,), (0,)), ((), ())), preferred_element_type=jnp.float32
    )


def exchange_kernel(jobs, *refs):
    count = len(jobs)
    sources, results = refs[:count], refs[count : 2 * count]
    sends, arrivals, keep = refs[2 * count :]
    axes = sorted({axis for axis, _ in jobs})
    barrier = pltpu.get_barrier_semaphore()
    greeted = 0
    for axis in axes:
        ways = lax.axis_size(axis)
        me = lax.axis_index(axis)
        for step in range(1, ways):
            pl.semaphore_signal(
                barrier,
                inc=1,
                device_id={axis: lax.rem(me + step, ways)},
                device_id_type=pl.DeviceIdType.MESH,
            )
        greeted += ways - 1
    pl.semaphore_wait(barrier, greeted)
    most = max(lax.axis_size(axis) for axis in axes)
    pending = []
    for step in range(1, most):
        for job, (axis, gather) in enumerate(jobs):
            ways = lax.axis_size(axis)
            if step >= ways:
                continue
            me = lax.axis_index(axis)
            peer = lax.rem(me + step, ways)
            copy = pltpu.make_async_remote_copy(
                src_ref=sources[job] if gather else sources[job].at[peer],
                dst_ref=results[job].at[me],
                send_sem=sends.at[job, step],
                recv_sem=arrivals.at[job, step],
                device_id={axis: peer},
                device_id_type=pl.DeviceIdType.MESH,
            )
            copy.start()
            pending.append(copy)
    for job, (axis, gather) in enumerate(jobs):
        me = lax.axis_index(axis)
        copy = pltpu.make_async_copy(
            sources[job] if gather else sources[job].at[me], results[job].at[me], keep.at[job]
        )
        copy.start()
        pending.append(copy)
    for copy in pending:
        copy.wait()


def exchange(collective_id, *jobs):
    shapes, sent = [], 0
    for array, axis, gather in jobs:
        block = array.shape if gather else array.shape[1:]
        ways = lax.axis_size(axis)
        shapes.append(jax.ShapeDtypeStruct((ways,) + block, array.dtype))
        sent += ways * array.dtype.itemsize * math.prod(block)
    most = max(lax.axis_size(axis) for _, axis, _ in jobs)
    count = len(jobs)
    return pl.pallas_call(
        functools.partial(exchange_kernel, tuple((axis, gather) for _, axis, gather in jobs)),
        out_shape=shapes,
        in_specs=[pl.BlockSpec(memory_space=pl.ANY)] * count,
        out_specs=[pl.BlockSpec(memory_space=pl.ANY)] * count,
        scratch_shapes=[
            pltpu.SemaphoreType.DMA((count, most)),
            pltpu.SemaphoreType.DMA((count, most)),
            pltpu.SemaphoreType.DMA((count,)),
        ],
        compiler_params=pltpu.CompilerParams(collective_id=collective_id, has_side_effects=True),
        cost_estimate=pl.CostEstimate(flops=0, bytes_accessed=2 * sent, transcendentals=0),
    )(*[array for array, _, _ in jobs])


def shards(
    student_cls,
    student_patches,
    teacher_cls,
    teacher_patches,
    mask_index,
    crop_pair,
    center,
    student_w1,
    student_w2,
    teacher_w1,
    teacher_w2,
    student_proto,
    teacher_proto,
):
    row_span = mask_index.shape[1] + 1
    masked_count = mask_index.shape[1]
    local_crops = student_cls.shape[0]
    proto_ways = lax.axis_size("proto")
    data_ways = lax.axis_size("dp")
    data_index = lax.axis_index("dp")
    crop_group = local_crops * proto_ways
    own_rows = local_crops * row_span
    group_rows = crop_group * row_span
    all_rows = group_rows * data_ways
    crops_total = crop_group * data_ways
    width = student_cls.shape[1]
    bottleneck = student_w2.shape[1]
    hidden_block = student_w1.shape[1]
    share = student_proto.shape[1] // data_ways

    rows_student = select_rows(student_cls, student_patches, mask_index)
    rows_teacher = select_rows(teacher_cls, teacher_patches, mask_index)
    pair_tile = jnp.broadcast_to(crop_pair[:, None, None], (local_crops, 8, 128))
    student_all, teacher_all, pairs, first_s, first_t = exchange(
        0,
        (rows_student, "proto", True),
        (rows_teacher, "proto", True),
        (pair_tile, "proto", True),
        (student_w1, "dp", True),
        (teacher_w1, "dp", True),
    )
    student_all = student_all.reshape(group_rows, width)
    teacher_all = teacher_all.reshape(group_rows, width)
    pairs = pairs[:, :, 0, 0].reshape(crop_group)

    preact = jnp.dot(
        student_all, first_s.reshape(width, hidden_block), preferred_element_type=jnp.float32
    )
    hidden = jax.nn.gelu(preact, approximate=False).astype(jnp.bfloat16)
    part_s = jnp.dot(hidden, student_w2, preferred_element_type=jnp.float32)
    teacher_pre = jnp.dot(
        teacher_all, first_t.reshape(width, hidden_block), preferred_element_type=jnp.float32
    )
    teacher_hidden = jax.nn.gelu(teacher_pre, approximate=False).astype(jnp.bfloat16)
    part_t = jnp.dot(teacher_hidden, teacher_w2, preferred_element_type=jnp.float32)
    by_crop = part_t.reshape(crop_group, row_span, bottleneck)
    by_crop = jnp.concatenate([by_crop[:, 0][pairs][:, None], by_crop[:, 1:]], axis=1)
    parts = jnp.concatenate([part_s, by_crop.reshape(group_rows, bottleneck)], axis=1)
    (parts,) = exchange(1, (parts.reshape(proto_ways, own_rows, 2 * bottleneck), "proto", False))
    bottles = jnp.sum(parts, axis=0)
    unit_s, inverse_s = normalize_rows(bottles[:, :bottleneck])
    unit_t, _ = normalize_rows(bottles[:, bottleneck:])
    packed = jnp.concatenate([unit_s, unit_t], axis=1).astype(jnp.bfloat16)
    (group_units,) = exchange(2, (packed, "proto", True))
    (all_units,) = exchange(3, (group_units.reshape(group_rows, 2 * bottleneck), "dp", True))
    all_units = all_units.reshape(all_rows, 2 * bottleneck)
    rows_s = all_units[:, :bottleneck]
    rows_t = all_units[:, bottleneck:]

    own_s = lax.dynamic_slice_in_dim(student_proto, data_index * share, share, axis=1)
    own_t = lax.dynamic_slice_in_dim(teacher_proto, data_index * share, share, axis=1)
    own_center = lax.dynamic_slice_in_dim(center, data_index * share, share, axis=1)
    proto_unit, col_inverse = normalize_columns(own_s)
    teacher_unit, _ = normalize_columns(own_t)
    proto_s_b = proto_unit.astype(jnp.bfloat16)
    proto_t_b = teacher_unit.astype(jnp.bfloat16)
    is_cls = jnp.arange(all_rows, dtype=jnp.int32) % row_span == 0
    shift = jnp.where(is_cls[:, None], own_center[0][None, :], own_center[1][None, :])
    logit_s = jnp.dot(rows_s, proto_s_b, preferred_element_type=jnp.float32) / student_temp
    logit_t = (
        jnp.dot(rows_t, proto_t_b, preferred_element_type=jnp.float32) - shift
    ) / teacher_temp
    exp_s = jnp.exp(logit_s)
    exp_t = jnp.exp(logit_t)
    sums = jnp.stack(
        [jnp.sum(exp_t, axis=1), jnp.sum(exp_s, axis=1), jnp.sum(exp_t * logit_s, axis=1)]
    )
    (sums,) = exchange(4, (sums.reshape(-1, 128), "proto", True))
    (sums,) = exchange(5, (jnp.sum(sums, axis=0), "dp", True))
    total_t, total_s, cross = jnp.sum(sums, axis=0).reshape(3, all_rows)
    weights = jnp.where(is_cls, 1.0 / crops_total, 1.0 / (crops_total * masked_count)).astype(
        jnp.float32
    )
    weighted_loss = weights * (jnp.log(total_s) - cross / total_t)
    loss_value = (
        jnp.sum(lax.dynamic_slice_in_dim(weighted_loss, data_index * group_rows, group_rows))
        * data_ways
    ).reshape(1)
    factor = loss_scale / student_temp * weights
    dscore = (
        exp_s * (factor / total_s)[:, None] - exp_t * (factor / total_t)[:, None]
    ).astype(jnp.bfloat16)
    grad_units = lax.dot_general(
        dscore, proto_s_b, (((1,), (1,)), ((), ())), preferred_element_type=jnp.float32
    )
    grad_cols = contract_rows(rows_s, dscore)
    projected = col_inverse * (
        grad_cols - proto_unit * jnp.sum(proto_unit * grad_cols, axis=0, keepdims=True)
    )
    (grad_units,) = exchange(
        6, (grad_units.reshape(data_ways, group_rows, bottleneck), "dp", False)
    )
    grad_units = jnp.sum(grad_units, axis=0).reshape(proto_ways, own_rows, bottleneck)
    projected = projected.astype(jnp.bfloat16).reshape(
        data_ways, bottleneck // data_ways, share
    )
    grad_units, projected = exchange(
        7, (grad_units, "proto", False), (projected, "dp", False)
    )
    grad_proto = (
        projected.transpose(1, 0, 2)
        .reshape(bottleneck // data_ways, data_ways * share)
        .astype(jnp.float32)
    )
    grad_units = jnp.sum(grad_units, axis=0)
    grad_z = (
        inverse_s * (grad_units - unit_s * jnp.sum(unit_s * grad_units, axis=1, keepdims=True))
    ).astype(jnp.bfloat16)
    (grad_z,) = exchange(8, (grad_z, "proto", True))
    grad_z = grad_z.reshape(group_rows, bottleneck)

    grad_hidden = lax.dot_general(
        grad_z, student_w2, (((1,), (1,)), ((), ())), preferred_element_type=jnp.float32
    )
    grad_pre = (grad_hidden * gelu_grad(preact)).astype(jnp.bfloat16)
    part_w1 = contract_rows(student_all, grad_pre).astype(jnp.bfloat16)
    part_w2 = contract_rows(hidden, grad_z).astype(jnp.bfloat16)
    part_w1, part_w2 = exchange(
        9,
        (part_w1.reshape(data_ways, width // data_ways, hidden_block), "dp", False),
        (part_w2, "dp", True),
    )
    grad_w1 = jnp.sum(part_w1.astype(jnp.float32), axis=0)
    grad_w2 = jnp.sum(part_w2.astype(jnp.float32), axis=0)
    return (loss_value, grad_w1, grad_w2, grad_proto)


def solution(mesh):
    placed = (
        P(("dp", "proto"), None),
        P(("dp", "proto"), None, None),
        P(("dp", "proto"), None),
        P(("dp", "proto"), None, None),
        P(("dp", "proto"), None),
        P(("dp", "proto")),
        P(None, "proto"),
        P("dp", "proto"),
        P("proto", None),
        P("dp", "proto"),
        P("proto", None),
        P(None, "proto"),
        P(None, "proto"),
    )
    return jax.shard_map(
        shards,
        mesh=mesh,
        in_specs=placed,
        out_specs=(P("dp"), P("dp", "proto"), P("proto", None), P("dp", "proto")),
        check_vma=False,
    )
```

```python
import functools
import math

import jax
import jax.numpy as jnp
from jax import lax
from jax.experimental import pallas as pl
from jax.experimental.pallas import tpu as pltpu
from jax.sharding import PartitionSpec as P

epsilon = 1e-06
teacher_temp = 0.07
student_temp = 0.1
loss_scale = 1048576.0
PROTO = ("proto",)
DATA = ("dp",)


def select_rows(cls_tokens, patches, mask_index):
    picked = jax.vmap(lambda patch_set, index_set: patch_set[index_set])(patches, mask_index)
    joined = jnp.concatenate([cls_tokens[:, None, :], picked], axis=1)
    return joined.reshape(-1, cls_tokens.shape[-1])


def normalize_rows(bottle):
    inverse = lax.rsqrt(jnp.sum(bottle * bottle, axis=-1, keepdims=True) + epsilon)
    return (bottle * inverse, inverse)


def normalize_columns(proto):
    inverse = lax.rsqrt(jnp.sum(proto * proto, axis=0, keepdims=True) + epsilon)
    return (proto * inverse, inverse)


def gelu_grad(preact):
    normal_cdf = 0.5 * (1.0 + lax.erf(preact * 0.7071067811865476))
    normal_pdf = jnp.exp(-0.5 * preact * preact) * 0.3989422804014327
    return normal_cdf + preact * normal_pdf


def contract_rows(left, right):
    return lax.dot_general(
        left, right, (((0,), (0,)), ((), ())), preferred_element_type=jnp.float32
    )


def place(rel):
    spot = {}
    for axis, (far, near) in rel.items():
        high, low = split_axis(axis)
        me = lax.axis_index(axis)
        spot[axis] = lax.rem(me // low + far, high) * low + lax.rem(me % low + near, low)
    return spot


def split_axis(axis):
    ways = lax.axis_size(axis)
    return (ways // 2, 2) if ways % 2 == 0 else (ways, 1)


def offsets(axes):
    found = [{axis: (0, 0) for axis in axes}]
    for axis in axes:
        high, low = split_axis(axis)
        found = [
            {**rel, axis: (far, near)}
            for far in range(high)
            for near in range(low)
            for rel in found
        ]
    return found


def key(rel):
    return tuple(sorted((axis, step) for axis, step in rel.items() if step != (0, 0)))


def steps_of(axes):
    return [
        (axis, part, split_axis(axis)[part])
        for axis in axes
        for part in (0, 1)
        if split_axis(axis)[part] > 1
    ]


def moved(rel, axis, part, offset):
    step = list(rel[axis])
    step[part] = offset
    return {**rel, axis: tuple(step)}


def slot(spot, axes):
    index = 0
    for axis in sorted(axes):
        index = index * lax.axis_size(axis) + spot[axis]
    return index


def exchange_kernel(jobs, *refs):
    count = len(jobs)
    sources, results = refs[:count], refs[count : 2 * count]
    sends, arrivals, keep = refs[2 * count :]
    peers = {}
    for axes, gather in jobs:
        if gather:
            own = {axis: (0, 0) for axis in axes}
            reached = [
                moved(own, axis, part, offset)
                for axis, part, size in steps_of(axes)
                for offset in range(1, size)
            ]
        else:
            reached = offsets(axes)[1:]
        for rel in reached:
            peers[key(rel)] = {axis: step for axis, step in rel.items() if step != (0, 0)}
    barrier = pltpu.get_barrier_semaphore()
    for rel in peers.values():
        pl.semaphore_signal(
            barrier, inc=1, device_id=place(rel), device_id_type=pl.DeviceIdType.MESH
        )
    pl.semaphore_wait(barrier, len(peers))

    sent = []
    held = [[{axis: (0, 0) for axis in axes}] for axes, _ in jobs]
    numbers = [{key(rel): n for n, rel in enumerate(offsets(axes))} for axes, _ in jobs]
    arriving = [{} for _ in jobs]

    def send(job, source, owner, to, number):
        copy = pltpu.make_async_remote_copy(
            src_ref=source,
            dst_ref=results[job].at[slot(owner, jobs[job][0])],
            send_sem=sends.at[job, number],
            recv_sem=arrivals.at[job, number],
            device_id=to,
            device_id_type=pl.DeviceIdType.MESH,
        )
        copy.start()
        sent.append(copy)

    def pass_on(job, rel, step):
        axis, part, size = step
        axes = jobs[job][0]
        if key(rel) in arriving[job]:
            arriving[job].pop(key(rel)).wait_recv()
        owner = place(rel)
        source = results[job].at[slot(owner, axes)] if key(rel) else sources[job]
        for offset in range(1, size):
            landed = moved(rel, axis, part, size - offset)
            to = place({axis: hop(part, offset)})
            send(job, source, owner, to, numbers[job][key(landed)])
            arriving[job][key(landed)] = copy_in(job, landed)

    def hop(part, offset):
        return (offset, 0) if part == 0 else (0, offset)

    def copy_in(job, landed):
        here = results[job].at[slot(place(landed), jobs[job][0])]
        number = numbers[job][key(landed)]
        return pltpu.make_async_remote_copy(
            src_ref=here,
            dst_ref=here,
            send_sem=sends.at[job, number],
            recv_sem=arrivals.at[job, number],
            device_id=place({axis: (0, 0) for axis in jobs[job][0]}),
            device_id_type=pl.DeviceIdType.MESH,
        )

    phases = [steps_of(axes) if gather else [] for axes, gather in jobs]
    local = []
    for phase in range(max([1] + [len(steps) for steps in phases])):
        before = [list(rels) for rels in held]
        for turn in range(max(len(rels) for rels in before)):
            for job, (axes, gather) in enumerate(jobs):
                if not gather or phase >= len(phases[job]) or turn >= len(before[job]):
                    continue
                axis, part, size = phases[job][phase]
                rel = before[job][turn]
                pass_on(job, rel, phases[job][phase])
                held[job] += [moved(rel, axis, part, size - offset) for offset in range(1, size)]
        if phase == 0:
            for job, (axes, gather) in enumerate(jobs):
                if not gather:
                    me = place({axis: (0, 0) for axis in axes})
                    for rel in offsets(axes)[1:]:
                        to = place(rel)
                        (axis,) = axes
                        high, low = split_axis(axis)
                        back = {axis: ((high - rel[axis][0]) % high, (low - rel[axis][1]) % low)}
                        number = numbers[job][key(back)]
                        send(job, sources[job].at[slot(to, axes)], me, to, number)
                        arriving[job][key(back)] = copy_in(job, back)
            for job, (axes, gather) in enumerate(jobs):
                me = slot(place({axis: (0, 0) for axis in axes}), axes)
                copy = pltpu.make_async_copy(
                    sources[job] if gather else sources[job].at[me],
                    results[job].at[me],
                    keep.at[job],
                )
                copy.start()
                local.append(copy)
    for waits in arriving:
        for copy in waits.values():
            copy.wait_recv()
    for copy in sent:
        copy.wait_send()
    for copy in local:
        copy.wait()


def exchange(collective_id, *jobs):
    shapes, moved_bytes = [], 0
    for array, axes, gather in jobs:
        block = array.shape if gather else array.shape[1:]
        ways = math.prod(lax.axis_size(axis) for axis in axes)
        shapes.append(jax.ShapeDtypeStruct((ways,) + block, array.dtype))
        moved_bytes += ways * array.dtype.itemsize * math.prod(block)
    most = max(shape.shape[0] for shape in shapes)
    count = len(jobs)
    return pl.pallas_call(
        functools.partial(exchange_kernel, tuple((axes, gather) for _, axes, gather in jobs)),
        out_shape=shapes,
        in_specs=[pl.BlockSpec(memory_space=pl.ANY)] * count,
        out_specs=[pl.BlockSpec(memory_space=pl.ANY)] * count,
        scratch_shapes=[
            pltpu.SemaphoreType.DMA((count, most)),
            pltpu.SemaphoreType.DMA((count, most)),
            pltpu.SemaphoreType.DMA((count,)),
        ],
        compiler_params=pltpu.CompilerParams(collective_id=collective_id, has_side_effects=True),
        cost_estimate=pl.CostEstimate(
            flops=0, bytes_accessed=2 * moved_bytes, transcendentals=0
        ),
    )(*[array for array, _, _ in jobs])


def shards(
    student_cls,
    student_patches,
    teacher_cls,
    teacher_patches,
    mask_index,
    crop_pair,
    center,
    student_w1,
    student_w2,
    teacher_w1,
    teacher_w2,
    student_proto,
    teacher_proto,
):
    row_span = mask_index.shape[1] + 1
    masked_count = mask_index.shape[1]
    local_crops = student_cls.shape[0]
    proto_ways = lax.axis_size("proto")
    data_ways = lax.axis_size("dp")
    data_index = lax.axis_index("dp")
    crop_group = local_crops * proto_ways
    own_rows = local_crops * row_span
    group_rows = crop_group * row_span
    all_rows = group_rows * data_ways
    crops_total = crop_group * data_ways
    width = student_cls.shape[1]
    bottleneck = student_w2.shape[1]
    hidden_block = student_w1.shape[1]
    share = student_proto.shape[1] // data_ways

    rows_student = select_rows(student_cls, student_patches, mask_index)
    rows_teacher = select_rows(teacher_cls, teacher_patches, mask_index)
    pair_tile = jnp.broadcast_to(crop_pair[:, None, None], (local_crops, 8, 128))
    student_all, teacher_all, pairs, first_s, first_t = exchange(
        0,
        (rows_student, PROTO, True),
        (rows_teacher, PROTO, True),
        (pair_tile, PROTO, True),
        (student_w1, DATA, True),
        (teacher_w1, DATA, True),
    )
    student_all = student_all.reshape(group_rows, width)
    teacher_all = teacher_all.reshape(group_rows, width)
    pairs = pairs[:, :, 0, 0].reshape(crop_group)

    preact = jnp.dot(
        student_all, first_s.reshape(width, hidden_block), preferred_element_type=jnp.float32
    )
    hidden = jax.nn.gelu(preact, approximate=False).astype(jnp.bfloat16)
    part_s = jnp.dot(hidden, student_w2, preferred_element_type=jnp.float32)
    teacher_pre = jnp.dot(
        teacher_all, first_t.reshape(width, hidden_block), preferred_element_type=jnp.float32
    )
    teacher_hidden = jax.nn.gelu(teacher_pre, approximate=False).astype(jnp.bfloat16)
    part_t = jnp.dot(teacher_hidden, teacher_w2, preferred_element_type=jnp.float32)
    by_crop = part_t.reshape(crop_group, row_span, bottleneck)
    by_crop = jnp.concatenate([by_crop[:, 0][pairs][:, None], by_crop[:, 1:]], axis=1)
    parts_s, parts_t = exchange(
        1,
        (part_s.reshape(proto_ways, own_rows, bottleneck), PROTO, False),
        (
            by_crop.astype(jnp.bfloat16).reshape(proto_ways, own_rows, bottleneck),
            PROTO,
            False,
        ),
    )
    unit_s, inverse_s = normalize_rows(jnp.sum(parts_s, axis=0))
    unit_t, _ = normalize_rows(jnp.sum(parts_t.astype(jnp.float32), axis=0))
    packed = jnp.concatenate([unit_s, unit_t], axis=1).astype(jnp.bfloat16)
    (all_units,) = exchange(2, (packed, PROTO + DATA, True))
    all_units = all_units.reshape(all_rows, 2 * bottleneck)
    rows_s = all_units[:, :bottleneck]
    rows_t = all_units[:, bottleneck:]

    own_s = lax.dynamic_slice_in_dim(student_proto, data_index * share, share, axis=1)
    own_t = lax.dynamic_slice_in_dim(teacher_proto, data_index * share, share, axis=1)
    own_center = lax.dynamic_slice_in_dim(center, data_index * share, share, axis=1)
    proto_unit, col_inverse = normalize_columns(own_s)
    teacher_unit, _ = normalize_columns(own_t)
    proto_s_b = proto_unit.astype(jnp.bfloat16)
    proto_t_b = teacher_unit.astype(jnp.bfloat16)
    is_cls = jnp.arange(all_rows, dtype=jnp.int32) % row_span == 0
    shift = jnp.where(is_cls[:, None], own_center[0][None, :], own_center[1][None, :])
    logit_s = jnp.dot(rows_s, proto_s_b, preferred_element_type=jnp.float32) / student_temp
    logit_t = (
        jnp.dot(rows_t, proto_t_b, preferred_element_type=jnp.float32) - shift
    ) / teacher_temp
    exp_s = jnp.exp(logit_s)
    exp_t = jnp.exp(logit_t)
    sums = jnp.stack(
        [jnp.sum(exp_t, axis=1), jnp.sum(exp_s, axis=1), jnp.sum(exp_t * logit_s, axis=1)]
    )
    (sums,) = exchange(3, (sums.reshape(-1, 128), PROTO + DATA, True))
    total_t, total_s, cross = jnp.sum(sums, axis=0).reshape(3, all_rows)
    weights = jnp.where(is_cls, 1.0 / crops_total, 1.0 / (crops_total * masked_count)).astype(
        jnp.float32
    )
    weighted_loss = weights * (jnp.log(total_s) - cross / total_t)
    loss_value = (
        jnp.sum(lax.dynamic_slice_in_dim(weighted_loss, data_index * group_rows, group_rows))
        * data_ways
    ).reshape(1)
    factor = loss_scale / student_temp * weights
    dscore = (
        exp_s * (factor / total_s)[:, None] - exp_t * (factor / total_t)[:, None]
    ).astype(jnp.bfloat16)
    grad_units = lax.dot_general(
        dscore, proto_s_b, (((1,), (1,)), ((), ())), preferred_element_type=jnp.float32
    )
    grad_cols = contract_rows(rows_s, dscore)
    projected = col_inverse * (
        grad_cols - proto_unit * jnp.sum(proto_unit * grad_cols, axis=0, keepdims=True)
    )
    (grad_units,) = exchange(
        4, (grad_units.reshape(data_ways, group_rows, bottleneck), DATA, False)
    )
    grad_units = jnp.sum(grad_units, axis=0).reshape(proto_ways, own_rows, bottleneck)
    projected = projected.astype(jnp.bfloat16).reshape(
        data_ways, bottleneck // data_ways, share
    )
    half = bottleneck // data_ways // 2
    grad_units, upper = exchange(
        5, (grad_units, PROTO, False), (projected[:, :half], DATA, False)
    )
    grad_units = jnp.sum(grad_units, axis=0)
    grad_z = (
        inverse_s * (grad_units - unit_s * jnp.sum(unit_s * grad_units, axis=1, keepdims=True))
    ).astype(jnp.bfloat16)
    grad_z, lower = exchange(6, (grad_z, PROTO, True), (projected[:, half:], DATA, False))
    grad_proto = (
        jnp.concatenate([upper, lower], axis=1)
        .transpose(1, 0, 2)
        .reshape(2 * half, data_ways * share)
        .astype(jnp.float32)
    )
    grad_z = grad_z.reshape(group_rows, bottleneck)

    grad_hidden = lax.dot_general(
        grad_z, student_w2, (((1,), (1,)), ((), ())), preferred_element_type=jnp.float32
    )
    grad_pre = (grad_hidden * gelu_grad(preact)).astype(jnp.bfloat16)
    part_w1 = contract_rows(student_all, grad_pre).astype(jnp.bfloat16)
    part_w2 = contract_rows(hidden, grad_z).astype(jnp.bfloat16)
    part_w1, part_w2 = exchange(
        7,
        (part_w1.reshape(data_ways, width // data_ways, hidden_block), DATA, False),
        (part_w2, DATA, True),
    )
    grad_w1 = jnp.sum(part_w1.astype(jnp.float32), axis=0)
    grad_w2 = jnp.sum(part_w2.astype(jnp.float32), axis=0)
    return (loss_value, grad_w1, grad_w2, grad_proto)


def solution(mesh):
    placed = (
        P(("dp", "proto"), None),
        P(("dp", "proto"), None, None),
        P(("dp", "proto"), None),
        P(("dp", "proto"), None, None),
        P(("dp", "proto"), None),
        P(("dp", "proto")),
        P(None, "proto"),
        P("dp", "proto"),
        P("proto", None),
        P("dp", "proto"),
        P("proto", None),
        P(None, "proto"),
        P(None, "proto"),
    )
    return jax.shard_map(
        shards,
        mesh=mesh,
        in_specs=placed,
        out_specs=(P("dp"), P("dp", "proto"), P("proto", None), P("dp", "proto")),
        check_vma=False,
    )
```

```python
import functools
import math

import jax
import jax.numpy as jnp
from jax import lax
from jax.experimental import pallas as pl
from jax.experimental.pallas import tpu as pltpu
from jax.sharding import PartitionSpec as P

epsilon = 1e-06
teacher_temp = 0.07
student_temp = 0.1
loss_scale = 1048576.0
PROTO = ("proto",)
DATA = ("dp",)


def select_rows(cls_tokens, patches, mask_index):
    picked = jax.vmap(lambda patch_set, index_set: patch_set[index_set])(patches, mask_index)
    joined = jnp.concatenate([cls_tokens[:, None, :], picked], axis=1)
    return joined.reshape(-1, cls_tokens.shape[-1])


def normalize_rows(bottle):
    inverse = lax.rsqrt(jnp.sum(bottle * bottle, axis=-1, keepdims=True) + epsilon)
    return (bottle * inverse, inverse)


def normalize_columns(proto):
    inverse = lax.rsqrt(jnp.sum(proto * proto, axis=0, keepdims=True) + epsilon)
    return (proto * inverse, inverse)


def gelu_grad(preact):
    normal_cdf = 0.5 * (1.0 + lax.erf(preact * 0.7071067811865476))
    normal_pdf = jnp.exp(-0.5 * preact * preact) * 0.3989422804014327
    return normal_cdf + preact * normal_pdf


def contract_rows(left, right):
    return lax.dot_general(
        left, right, (((0,), (0,)), ((), ())), preferred_element_type=jnp.float32
    )


def place(rel):
    spot = {}
    for axis, (far, near) in rel.items():
        high, low = split_axis(axis)
        me = lax.axis_index(axis)
        spot[axis] = lax.rem(me // low + far, high) * low + lax.rem(me % low + near, low)
    return spot


def split_axis(axis):
    ways = lax.axis_size(axis)
    return (ways // 2, 2) if ways % 2 == 0 else (ways, 1)


def offsets(axes):
    found = [{axis: (0, 0) for axis in axes}]
    for axis in axes:
        high, low = split_axis(axis)
        found = [
            {**rel, axis: (far, near)}
            for far in range(high)
            for near in range(low)
            for rel in found
        ]
    return found


def key(rel):
    return tuple(sorted((axis, step) for axis, step in rel.items() if step != (0, 0)))


def steps_of(axes):
    return [
        (axis, part, split_axis(axis)[part])
        for axis in axes
        for part in (0, 1)
        if split_axis(axis)[part] > 1
    ]


def moved(rel, axis, part, offset):
    step = list(rel[axis])
    step[part] = offset
    return {**rel, axis: tuple(step)}


def slot(spot, axes):
    index = 0
    for axis in sorted(axes):
        index = index * lax.axis_size(axis) + spot[axis]
    return index


def exchange_kernel(jobs, *refs):
    count = len(jobs)
    sources, results = refs[:count], refs[count : 2 * count]
    sends, arrivals, keep = refs[2 * count :]
    peers = {}
    for axes, gather in jobs:
        if gather:
            own = {axis: (0, 0) for axis in axes}
            reached = [
                moved(own, axis, part, offset)
                for axis, part, size in steps_of(axes)
                for offset in range(1, size)
            ]
        else:
            reached = offsets(axes)[1:]
        for rel in reached:
            peers[key(rel)] = {axis: step for axis, step in rel.items() if step != (0, 0)}
    barrier = pltpu.get_barrier_semaphore()
    for rel in peers.values():
        pl.semaphore_signal(
            barrier, inc=1, device_id=place(rel), device_id_type=pl.DeviceIdType.MESH
        )
    pl.semaphore_wait(barrier, len(peers))

    sent = []
    held = [[{axis: (0, 0) for axis in axes}] for axes, _ in jobs]
    numbers = [{key(rel): n for n, rel in enumerate(offsets(axes))} for axes, _ in jobs]
    arriving = [{} for _ in jobs]

    def send(job, source, owner, to, number):
        copy = pltpu.make_async_remote_copy(
            src_ref=source,
            dst_ref=results[job].at[slot(owner, jobs[job][0])],
            send_sem=sends.at[job, number],
            recv_sem=arrivals.at[job, number],
            device_id=to,
            device_id_type=pl.DeviceIdType.MESH,
        )
        copy.start()
        sent.append(copy)

    def pass_on(job, rel, step):
        axis, part, size = step
        axes = jobs[job][0]
        if key(rel) in arriving[job]:
            arriving[job].pop(key(rel)).wait_recv()
        owner = place(rel)
        source = results[job].at[slot(owner, axes)] if key(rel) else sources[job]
        for offset in range(1, size):
            landed = moved(rel, axis, part, size - offset)
            to = place({axis: hop(part, offset)})
            send(job, source, owner, to, numbers[job][key(landed)])
            arriving[job][key(landed)] = copy_in(job, landed)

    def hop(part, offset):
        return (offset, 0) if part == 0 else (0, offset)

    def copy_in(job, landed):
        here = results[job].at[slot(place(landed), jobs[job][0])]
        number = numbers[job][key(landed)]
        return pltpu.make_async_remote_copy(
            src_ref=here,
            dst_ref=here,
            send_sem=sends.at[job, number],
            recv_sem=arrivals.at[job, number],
            device_id=place({axis: (0, 0) for axis in jobs[job][0]}),
            device_id_type=pl.DeviceIdType.MESH,
        )

    phases = [steps_of(axes) if gather else [] for axes, gather in jobs]
    local = []
    for phase in range(max([1] + [len(steps) for steps in phases])):
        before = [list(rels) for rels in held]
        for turn in range(max(len(rels) for rels in before)):
            for job, (axes, gather) in enumerate(jobs):
                if not gather or phase >= len(phases[job]) or turn >= len(before[job]):
                    continue
                axis, part, size = phases[job][phase]
                rel = before[job][turn]
                pass_on(job, rel, phases[job][phase])
                held[job] += [moved(rel, axis, part, size - offset) for offset in range(1, size)]
        if phase == 0:
            for job, (axes, gather) in enumerate(jobs):
                if not gather:
                    me = place({axis: (0, 0) for axis in axes})
                    for rel in offsets(axes)[1:]:
                        to = place(rel)
                        (axis,) = axes
                        high, low = split_axis(axis)
                        back = {axis: ((high - rel[axis][0]) % high, (low - rel[axis][1]) % low)}
                        number = numbers[job][key(back)]
                        send(job, sources[job].at[slot(to, axes)], me, to, number)
                        arriving[job][key(back)] = copy_in(job, back)
            for job, (axes, gather) in enumerate(jobs):
                me = slot(place({axis: (0, 0) for axis in axes}), axes)
                copy = pltpu.make_async_copy(
                    sources[job] if gather else sources[job].at[me],
                    results[job].at[me],
                    keep.at[job],
                )
                copy.start()
                local.append(copy)
    for waits in arriving:
        for copy in waits.values():
            copy.wait_recv()
    for copy in sent:
        copy.wait_send()
    for copy in local:
        copy.wait()


def exchange(collective_id, *jobs):
    shapes, moved_bytes = [], 0
    for array, axes, gather in jobs:
        block = array.shape if gather else array.shape[1:]
        ways = math.prod(lax.axis_size(axis) for axis in axes)
        shapes.append(jax.ShapeDtypeStruct((ways,) + block, array.dtype))
        moved_bytes += ways * array.dtype.itemsize * math.prod(block)
    most = max(shape.shape[0] for shape in shapes)
    count = len(jobs)
    return pl.pallas_call(
        functools.partial(exchange_kernel, tuple((axes, gather) for _, axes, gather in jobs)),
        out_shape=shapes,
        in_specs=[pl.BlockSpec(memory_space=pl.ANY)] * count,
        out_specs=[pl.BlockSpec(memory_space=pl.ANY)] * count,
        scratch_shapes=[
            pltpu.SemaphoreType.DMA((count, most)),
            pltpu.SemaphoreType.DMA((count, most)),
            pltpu.SemaphoreType.DMA((count,)),
        ],
        compiler_params=pltpu.CompilerParams(collective_id=collective_id, has_side_effects=True),
        cost_estimate=pl.CostEstimate(
            flops=0, bytes_accessed=2 * moved_bytes, transcendentals=0
        ),
    )(*[array for array, _, _ in jobs])


def score_kernel(row_span, zs_ref, zt_ref, ps_ref, pt_ref, center_ref, es_ref, et_ref, sums_ref):
    rows, share = es_ref.shape
    chunk = min(512, share)
    row = lax.broadcasted_iota(jnp.int32, (rows, 1), 0)
    is_cls = lax.rem(row, row_span) == 0
    total_t = jnp.zeros((rows, chunk), jnp.float32)
    total_s = jnp.zeros((rows, chunk), jnp.float32)
    cross = jnp.zeros((rows, chunk), jnp.float32)
    for start in range(0, share, chunk):
        here = pl.ds(start, chunk)
        logit_s = jnp.dot(
            zs_ref[...], ps_ref[:, here], preferred_element_type=jnp.float32
        ) * (1.0 / student_temp)
        shift = jnp.where(is_cls, center_ref[0:1, here], center_ref[1:2, here])
        logit_t = (
            jnp.dot(zt_ref[...], pt_ref[:, here], preferred_element_type=jnp.float32) - shift
        ) * (1.0 / teacher_temp)
        exp_s = jnp.exp(logit_s)
        exp_t = jnp.exp(logit_t)
        es_ref[:, here] = exp_s
        et_ref[:, here] = exp_t
        total_t += exp_t
        total_s += exp_s
        cross += exp_t * logit_s
    lane = lax.broadcasted_iota(jnp.int32, (rows, 128), 1)
    sums_ref[...] = jnp.where(
        lane == 0,
        jnp.sum(total_t, axis=1, keepdims=True),
        jnp.where(
            lane == 1,
            jnp.sum(total_s, axis=1, keepdims=True),
            jnp.sum(cross, axis=1, keepdims=True),
        ),
    )


def scores(rows_s, rows_t, proto_s, proto_t, center, row_span):
    rows, depth = rows_s.shape
    share = proto_s.shape[1]
    tile = math.gcd(rows, 8 * row_span)
    return pl.pallas_call(
        functools.partial(score_kernel, row_span),
        grid=(rows // tile,),
        out_shape=[
            jax.ShapeDtypeStruct((rows, share), jnp.float32),
            jax.ShapeDtypeStruct((rows, share), jnp.float32),
            jax.ShapeDtypeStruct((rows, 128), jnp.float32),
        ],
        in_specs=[
            pl.BlockSpec((tile, depth), lambda i: (i, 0)),
            pl.BlockSpec((tile, depth), lambda i: (i, 0)),
            pl.BlockSpec((depth, share), lambda i: (0, 0)),
            pl.BlockSpec((depth, share), lambda i: (0, 0)),
            pl.BlockSpec((2, share), lambda i: (0, 0)),
        ],
        out_specs=[
            pl.BlockSpec((tile, share), lambda i: (i, 0)),
            pl.BlockSpec((tile, share), lambda i: (i, 0)),
            pl.BlockSpec((tile, 128), lambda i: (i, 0)),
        ],
        compiler_params=pltpu.CompilerParams(vmem_limit_bytes=48 * 2**20),
    )(rows_s, rows_t, proto_s, proto_t, center)


def gradient_kernel(
    zs_ref, ps_ref, unit_ref, inverse_ref, es_ref, et_ref, scale_ref, units_ref, out_ref, cols_ref
):
    rows, share = es_ref.shape
    chunk = min(512, share)
    scale_s = scale_ref[:, 0:1]
    scale_t = scale_ref[:, 1:2]
    step = pl.program_id(0)

    @pl.when(step == 0)
    def _():
        cols_ref[...] = jnp.zeros_like(cols_ref)

    total = jnp.zeros(units_ref.shape, jnp.float32)
    for start in range(0, share, chunk):
        here = pl.ds(start, chunk)
        dscore = (es_ref[:, here] * scale_s - et_ref[:, here] * scale_t).astype(jnp.bfloat16)
        total += lax.dot_general(
            dscore, ps_ref[:, here], (((1,), (1,)), ((), ())), preferred_element_type=jnp.float32
        )
        cols_ref[:, here] += contract_rows(zs_ref[...], dscore)
    units_ref[...] = total

    @pl.when(step == pl.num_programs(0) - 1)
    def _():
        for start in range(0, share, chunk):
            here = pl.ds(start, chunk)
            cols = cols_ref[:, here]
            unit = unit_ref[:, here]
            along = jnp.sum(unit * cols, axis=0, keepdims=True)
            out_ref[:, here] = (inverse_ref[:, here] * (cols - unit * along)).astype(jnp.bfloat16)


def gradients(rows_s, proto_s, proto_unit, col_inverse, exp_s, exp_t, scales, row_span):
    rows, depth = rows_s.shape
    share = proto_s.shape[1]
    tile = math.gcd(rows, 8 * row_span)
    return pl.pallas_call(
        gradient_kernel,
        grid=(rows // tile,),
        out_shape=[
            jax.ShapeDtypeStruct((rows, depth), jnp.float32),
            jax.ShapeDtypeStruct((depth, share), jnp.bfloat16),
        ],
        in_specs=[
            pl.BlockSpec((tile, depth), lambda i: (i, 0)),
            pl.BlockSpec((depth, share), lambda i: (0, 0)),
            pl.BlockSpec((depth, share), lambda i: (0, 0)),
            pl.BlockSpec((1, share), lambda i: (0, 0)),
            pl.BlockSpec((tile, share), lambda i: (i, 0)),
            pl.BlockSpec((tile, share), lambda i: (i, 0)),
            pl.BlockSpec((tile, 2), lambda i: (i, 0)),
        ],
        out_specs=[
            pl.BlockSpec((tile, depth), lambda i: (i, 0)),
            pl.BlockSpec((depth, share), lambda i: (0, 0)),
        ],
        scratch_shapes=[pltpu.VMEM((depth, share), jnp.float32)],
        compiler_params=pltpu.CompilerParams(vmem_limit_bytes=48 * 2**20),
    )(rows_s, proto_s, proto_unit, col_inverse, exp_s, exp_t, scales)


def shards(
    student_cls,
    student_patches,
    teacher_cls,
    teacher_patches,
    mask_index,
    crop_pair,
    center,
    student_w1,
    student_w2,
    teacher_w1,
    teacher_w2,
    student_proto,
    teacher_proto,
):
    row_span = mask_index.shape[1] + 1
    masked_count = mask_index.shape[1]
    local_crops = student_cls.shape[0]
    proto_ways = lax.axis_size("proto")
    data_ways = lax.axis_size("dp")
    data_index = lax.axis_index("dp")
    crop_group = local_crops * proto_ways
    own_rows = local_crops * row_span
    group_rows = crop_group * row_span
    all_rows = group_rows * data_ways
    crops_total = crop_group * data_ways
    width = student_cls.shape[1]
    bottleneck = student_w2.shape[1]
    hidden_block = student_w1.shape[1]
    share = student_proto.shape[1] // data_ways

    rows_student = select_rows(student_cls, student_patches, mask_index)
    rows_teacher = select_rows(teacher_cls, teacher_patches, mask_index)
    pair_tile = jnp.broadcast_to(crop_pair[:, None, None], (local_crops, 8, 128))
    student_all, teacher_all, pairs, first_s, first_t = exchange(
        0,
        (rows_student, PROTO, True),
        (rows_teacher, PROTO, True),
        (pair_tile, PROTO, True),
        (student_w1, DATA, True),
        (teacher_w1, DATA, True),
    )
    student_all = student_all.reshape(group_rows, width)
    teacher_all = teacher_all.reshape(group_rows, width)
    pairs = pairs[:, :, 0, 0].reshape(crop_group)

    preact = jnp.dot(
        student_all, first_s.reshape(width, hidden_block), preferred_element_type=jnp.float32
    )
    hidden = jax.nn.gelu(preact, approximate=False).astype(jnp.bfloat16)
    part_s = jnp.dot(hidden, student_w2, preferred_element_type=jnp.float32)
    teacher_pre = jnp.dot(
        teacher_all, first_t.reshape(width, hidden_block), preferred_element_type=jnp.float32
    )
    teacher_hidden = jax.nn.gelu(teacher_pre, approximate=False).astype(jnp.bfloat16)
    part_t = jnp.dot(teacher_hidden, teacher_w2, preferred_element_type=jnp.float32)
    by_crop = part_t.reshape(crop_group, row_span, bottleneck)
    by_crop = jnp.concatenate([by_crop[:, 0][pairs][:, None], by_crop[:, 1:]], axis=1)
    parts_s, parts_t = exchange(
        1,
        (part_s.reshape(proto_ways, own_rows, bottleneck), PROTO, False),
        (
            by_crop.astype(jnp.bfloat16).reshape(proto_ways, own_rows, bottleneck),
            PROTO,
            False,
        ),
    )
    unit_s, inverse_s = normalize_rows(jnp.sum(parts_s, axis=0))
    unit_t, _ = normalize_rows(jnp.sum(parts_t.astype(jnp.float32), axis=0))
    packed = jnp.concatenate([unit_s, unit_t], axis=1).astype(jnp.bfloat16)
    (all_units,) = exchange(2, (packed, PROTO + DATA, True))
    all_units = all_units.reshape(all_rows, 2 * bottleneck)
    rows_s = all_units[:, :bottleneck]
    rows_t = all_units[:, bottleneck:]

    own_s = lax.dynamic_slice_in_dim(student_proto, data_index * share, share, axis=1)
    own_t = lax.dynamic_slice_in_dim(teacher_proto, data_index * share, share, axis=1)
    own_center = lax.dynamic_slice_in_dim(center, data_index * share, share, axis=1)
    proto_unit, col_inverse = normalize_columns(own_s)
    teacher_unit, _ = normalize_columns(own_t)
    proto_s_b = proto_unit.astype(jnp.bfloat16)
    proto_t_b = teacher_unit.astype(jnp.bfloat16)
    is_cls = jnp.arange(all_rows, dtype=jnp.int32) % row_span == 0
    exp_s, exp_t, sums = scores(rows_s, rows_t, proto_s_b, proto_t_b, own_center, row_span)
    sums = sums[:, :3].T
    (sums,) = exchange(3, (sums.reshape(-1, 128), PROTO + DATA, True))
    total_t, total_s, cross = jnp.sum(sums, axis=0).reshape(3, all_rows)
    weights = jnp.where(is_cls, 1.0 / crops_total, 1.0 / (crops_total * masked_count)).astype(
        jnp.float32
    )
    weighted_loss = weights * (jnp.log(total_s) - cross / total_t)
    loss_value = (
        jnp.sum(lax.dynamic_slice_in_dim(weighted_loss, data_index * group_rows, group_rows))
        * data_ways
    ).reshape(1)
    factor = loss_scale / student_temp * weights
    scales = jnp.stack([factor / total_s, factor / total_t], axis=1)
    grad_units, projected = gradients(
        rows_s, proto_s_b, proto_unit, col_inverse, exp_s, exp_t, scales, row_span
    )
    (grad_units,) = exchange(
        4, (grad_units.reshape(data_ways, group_rows, bottleneck), DATA, False)
    )
    grad_units = jnp.sum(grad_units, axis=0).reshape(proto_ways, own_rows, bottleneck)
    projected = projected.reshape(
        data_ways, bottleneck // data_ways, share
    )
    half = bottleneck // data_ways // 2
    grad_units, upper = exchange(
        5, (grad_units, PROTO, False), (projected[:, :half], DATA, False)
    )
    grad_units = jnp.sum(grad_units, axis=0)
    grad_z = (
        inverse_s * (grad_units - unit_s * jnp.sum(unit_s * grad_units, axis=1, keepdims=True))
    ).astype(jnp.bfloat16)
    grad_z, lower = exchange(6, (grad_z, PROTO, True), (projected[:, half:], DATA, False))
    grad_proto = (
        jnp.concatenate([upper, lower], axis=1)
        .transpose(1, 0, 2)
        .reshape(2 * half, data_ways * share)
        .astype(jnp.float32)
    )
    grad_z = grad_z.reshape(group_rows, bottleneck)

    grad_hidden = lax.dot_general(
        grad_z, student_w2, (((1,), (1,)), ((), ())), preferred_element_type=jnp.float32
    )
    grad_pre = (grad_hidden * gelu_grad(preact)).astype(jnp.bfloat16)
    part_w1 = contract_rows(student_all, grad_pre).astype(jnp.bfloat16)
    part_w2 = contract_rows(hidden, grad_z).astype(jnp.bfloat16)
    part_w1, part_w2 = exchange(
        7,
        (part_w1.reshape(data_ways, width // data_ways, hidden_block), DATA, False),
        (part_w2, DATA, True),
    )
    grad_w1 = jnp.sum(part_w1.astype(jnp.float32), axis=0)
    grad_w2 = jnp.sum(part_w2.astype(jnp.float32), axis=0)
    return (loss_value, grad_w1, grad_w2, grad_proto)


def solution(mesh):
    placed = (
        P(("dp", "proto"), None),
        P(("dp", "proto"), None, None),
        P(("dp", "proto"), None),
        P(("dp", "proto"), None, None),
        P(("dp", "proto"), None),
        P(("dp", "proto")),
        P(None, "proto"),
        P("dp", "proto"),
        P("proto", None),
        P("dp", "proto"),
        P("proto", None),
        P(None, "proto"),
        P(None, "proto"),
    )
    return jax.shard_map(
        shards,
        mesh=mesh,
        in_specs=placed,
        out_specs=(P("dp"), P("dp", "proto"), P("proto", None), P("dp", "proto")),
        check_vma=False,
    )
```

```python
import functools
import math

import jax
import jax.numpy as jnp
from jax import lax
from jax.experimental import pallas as pl
from jax.experimental.pallas import tpu as pltpu
from jax.sharding import PartitionSpec as P

epsilon = 1e-06
teacher_temp = 0.07
student_temp = 0.1
loss_scale = 1048576.0
PROTO = ("proto",)
DATA = ("dp",)


def select_rows(cls_tokens, patches, mask_index):
    picked = jax.vmap(lambda patch_set, index_set: patch_set[index_set])(patches, mask_index)
    joined = jnp.concatenate([cls_tokens[:, None, :], picked], axis=1)
    return joined.reshape(-1, cls_tokens.shape[-1])


def normalize_rows(bottle):
    inverse = lax.rsqrt(jnp.sum(bottle * bottle, axis=-1, keepdims=True) + epsilon)
    return (bottle * inverse, inverse)


def normalize_columns(proto):
    inverse = lax.rsqrt(jnp.sum(proto * proto, axis=0, keepdims=True) + epsilon)
    return (proto * inverse, inverse)


def gelu_grad(preact):
    normal_cdf = 0.5 * (1.0 + lax.erf(preact * 0.7071067811865476))
    normal_pdf = jnp.exp(-0.5 * preact * preact) * 0.3989422804014327
    return normal_cdf + preact * normal_pdf


def contract_rows(left, right):
    return lax.dot_general(
        left, right, (((0,), (0,)), ((), ())), preferred_element_type=jnp.float32
    )


def place(rel):
    spot = {}
    for axis, (far, near) in rel.items():
        high, low = split_axis(axis)
        me = lax.axis_index(axis)
        spot[axis] = lax.rem(me // low + far, high) * low + lax.rem(me % low + near, low)
    return spot


def split_axis(axis):
    ways = lax.axis_size(axis)
    return (ways // 2, 2) if ways % 2 == 0 else (ways, 1)


def offsets(axes):
    found = [{axis: (0, 0) for axis in axes}]
    for axis in axes:
        high, low = split_axis(axis)
        found = [
            {**rel, axis: (far, near)}
            for far in range(high)
            for near in range(low)
            for rel in found
        ]
    return found


def key(rel):
    return tuple(sorted((axis, step) for axis, step in rel.items() if step != (0, 0)))


def steps_of(axes):
    return [
        (axis, part, split_axis(axis)[part])
        for axis in axes
        for part in (0, 1)
        if split_axis(axis)[part] > 1
    ]


def moved(rel, axis, part, offset):
    step = list(rel[axis])
    step[part] = offset
    return {**rel, axis: tuple(step)}


def slot(spot, axes):
    index = 0
    for axis in sorted(axes):
        index = index * lax.axis_size(axis) + spot[axis]
    return index


def exchange_kernel(jobs, *refs):
    count = len(jobs)
    sources, results = refs[:count], refs[count : 2 * count]
    sends, arrivals, keep = refs[2 * count :]
    peers = {}
    for axes, gather in jobs:
        if gather:
            own = {axis: (0, 0) for axis in axes}
            reached = [
                moved(own, axis, part, offset)
                for axis, part, size in steps_of(axes)
                for offset in range(1, size)
            ]
        else:
            reached = offsets(axes)[1:]
        for rel in reached:
            peers[key(rel)] = {axis: step for axis, step in rel.items() if step != (0, 0)}
    barrier = pltpu.get_barrier_semaphore()
    for rel in peers.values():
        pl.semaphore_signal(
            barrier, inc=1, device_id=place(rel), device_id_type=pl.DeviceIdType.MESH
        )
    pl.semaphore_wait(barrier, len(peers))

    sent = []
    held = [[{axis: (0, 0) for axis in axes}] for axes, _ in jobs]
    numbers = [{key(rel): n for n, rel in enumerate(offsets(axes))} for axes, _ in jobs]
    arriving = [{} for _ in jobs]

    def send(job, source, owner, to, number):
        copy = pltpu.make_async_remote_copy(
            src_ref=source,
            dst_ref=results[job].at[slot(owner, jobs[job][0])],
            send_sem=sends.at[job, number],
            recv_sem=arrivals.at[job, number],
            device_id=to,
            device_id_type=pl.DeviceIdType.MESH,
        )
        copy.start()
        sent.append(copy)

    def pass_on(job, rel, step):
        axis, part, size = step
        axes = jobs[job][0]
        if key(rel) in arriving[job]:
            arriving[job].pop(key(rel)).wait_recv()
        owner = place(rel)
        source = results[job].at[slot(owner, axes)] if key(rel) else sources[job]
        for offset in range(1, size):
            landed = moved(rel, axis, part, size - offset)
            to = place({axis: hop(part, offset)})
            send(job, source, owner, to, numbers[job][key(landed)])
            arriving[job][key(landed)] = copy_in(job, landed)

    def hop(part, offset):
        return (offset, 0) if part == 0 else (0, offset)

    def copy_in(job, landed):
        here = results[job].at[slot(place(landed), jobs[job][0])]
        number = numbers[job][key(landed)]
        return pltpu.make_async_remote_copy(
            src_ref=here,
            dst_ref=here,
            send_sem=sends.at[job, number],
            recv_sem=arrivals.at[job, number],
            device_id=place({axis: (0, 0) for axis in jobs[job][0]}),
            device_id_type=pl.DeviceIdType.MESH,
        )

    phases = [steps_of(axes) if gather else [] for axes, gather in jobs]
    local = []
    for phase in range(max([1] + [len(steps) for steps in phases])):
        before = [list(rels) for rels in held]
        for turn in range(max(len(rels) for rels in before)):
            for job, (axes, gather) in enumerate(jobs):
                if not gather or phase >= len(phases[job]) or turn >= len(before[job]):
                    continue
                axis, part, size = phases[job][phase]
                rel = before[job][turn]
                pass_on(job, rel, phases[job][phase])
                held[job] += [moved(rel, axis, part, size - offset) for offset in range(1, size)]
        if phase == 0:
            for job, (axes, gather) in enumerate(jobs):
                if not gather:
                    me = place({axis: (0, 0) for axis in axes})
                    for rel in offsets(axes)[1:]:
                        to = place(rel)
                        (axis,) = axes
                        high, low = split_axis(axis)
                        back = {axis: ((high - rel[axis][0]) % high, (low - rel[axis][1]) % low)}
                        number = numbers[job][key(back)]
                        send(job, sources[job].at[slot(to, axes)], me, to, number)
                        arriving[job][key(back)] = copy_in(job, back)
            for job, (axes, gather) in enumerate(jobs):
                me = slot(place({axis: (0, 0) for axis in axes}), axes)
                copy = pltpu.make_async_copy(
                    sources[job] if gather else sources[job].at[me],
                    results[job].at[me],
                    keep.at[job],
                )
                copy.start()
                local.append(copy)
    for waits in arriving:
        for copy in waits.values():
            copy.wait_recv()
    for copy in sent:
        copy.wait_send()
    for copy in local:
        copy.wait()


def exchange(collective_id, *jobs):
    shapes, moved_bytes = [], 0
    for array, axes, gather in jobs:
        block = array.shape if gather else array.shape[1:]
        ways = math.prod(lax.axis_size(axis) for axis in axes)
        shapes.append(jax.ShapeDtypeStruct((ways,) + block, array.dtype))
        moved_bytes += ways * array.dtype.itemsize * math.prod(block)
    most = max(shape.shape[0] for shape in shapes)
    count = len(jobs)
    return pl.pallas_call(
        functools.partial(exchange_kernel, tuple((axes, gather) for _, axes, gather in jobs)),
        out_shape=shapes,
        in_specs=[pl.BlockSpec(memory_space=pl.ANY)] * count,
        out_specs=[pl.BlockSpec(memory_space=pl.ANY)] * count,
        scratch_shapes=[
            pltpu.SemaphoreType.DMA((count, most)),
            pltpu.SemaphoreType.DMA((count, most)),
            pltpu.SemaphoreType.DMA((count,)),
        ],
        compiler_params=pltpu.CompilerParams(collective_id=collective_id, has_side_effects=True),
        cost_estimate=pl.CostEstimate(
            flops=0, bytes_accessed=2 * moved_bytes, transcendentals=0
        ),
    )(*[array for array, _, _ in jobs])


def score_kernel(row_span, zs_ref, zt_ref, ps_ref, pt_ref, center_ref, es_ref, et_ref, sums_ref):
    rows, share = es_ref.shape
    chunk = min(512, share)
    row = lax.broadcasted_iota(jnp.int32, (rows, 1), 0)
    is_cls = lax.rem(row, row_span) == 0
    total_t = jnp.zeros((rows, chunk), jnp.float32)
    total_s = jnp.zeros((rows, chunk), jnp.float32)
    cross = jnp.zeros((rows, chunk), jnp.float32)
    for start in range(0, share, chunk):
        here = pl.ds(start, chunk)
        logit_s = jnp.dot(
            zs_ref[...], ps_ref[:, here], preferred_element_type=jnp.float32
        ) * (1.0 / student_temp)
        shift = jnp.where(is_cls, center_ref[0:1, here], center_ref[1:2, here])
        logit_t = (
            jnp.dot(zt_ref[...], pt_ref[:, here], preferred_element_type=jnp.float32) - shift
        ) * (1.0 / teacher_temp)
        exp_s = jnp.exp(logit_s)
        exp_t = jnp.exp(logit_t)
        es_ref[:, here] = exp_s
        et_ref[:, here] = exp_t
        total_t += exp_t
        total_s += exp_s
        cross += exp_t * logit_s
    lane = lax.broadcasted_iota(jnp.int32, (rows, 128), 1)
    sums_ref[...] = jnp.where(
        lane == 0,
        jnp.sum(total_t, axis=1, keepdims=True),
        jnp.where(
            lane == 1,
            jnp.sum(total_s, axis=1, keepdims=True),
            jnp.sum(cross, axis=1, keepdims=True),
        ),
    )


def scores(units, proto_s, proto_t, center, row_span):
    rows = units.shape[0]
    depth, share = proto_s.shape
    tile = math.gcd(rows, 8 * row_span)
    return pl.pallas_call(
        functools.partial(score_kernel, row_span),
        grid=(rows // tile,),
        out_shape=[
            jax.ShapeDtypeStruct((rows, share), jnp.float32),
            jax.ShapeDtypeStruct((rows, share), jnp.float32),
            jax.ShapeDtypeStruct((rows, 128), jnp.float32),
        ],
        in_specs=[
            pl.BlockSpec((tile, depth), lambda i: (i, 0)),
            pl.BlockSpec((tile, depth), lambda i: (i, 1)),
            pl.BlockSpec((depth, share), lambda i: (0, 0)),
            pl.BlockSpec((depth, share), lambda i: (0, 0)),
            pl.BlockSpec((2, share), lambda i: (0, 0)),
        ],
        out_specs=[
            pl.BlockSpec((tile, share), lambda i: (i, 0)),
            pl.BlockSpec((tile, share), lambda i: (i, 0)),
            pl.BlockSpec((tile, 128), lambda i: (i, 0)),
        ],
        compiler_params=pltpu.CompilerParams(vmem_limit_bytes=48 * 2**20),
    )(units, units, proto_s, proto_t, center)


def gradient_kernel(
    zs_ref, ps_ref, unit_ref, inverse_ref, es_ref, et_ref, scale_ref, units_ref, out_ref, cols_ref
):
    rows, share = es_ref.shape
    chunk = min(512, share)
    scale_s = scale_ref[:, 0:1]
    scale_t = scale_ref[:, 1:2]
    step = pl.program_id(0)

    @pl.when(step == 0)
    def _():
        cols_ref[...] = jnp.zeros_like(cols_ref)

    total = jnp.zeros(units_ref.shape, jnp.float32)
    for start in range(0, share, chunk):
        here = pl.ds(start, chunk)
        dscore = (es_ref[:, here] * scale_s - et_ref[:, here] * scale_t).astype(jnp.bfloat16)
        total += lax.dot_general(
            dscore, ps_ref[:, here], (((1,), (1,)), ((), ())), preferred_element_type=jnp.float32
        )
        cols_ref[:, here] += contract_rows(zs_ref[...], dscore)
    units_ref[...] = total

    @pl.when(step == pl.num_programs(0) - 1)
    def _():
        for start in range(0, share, chunk):
            here = pl.ds(start, chunk)
            cols = cols_ref[:, here]
            unit = unit_ref[:, here]
            along = jnp.sum(unit * cols, axis=0, keepdims=True)
            out_ref[:, here] = (inverse_ref[:, here] * (cols - unit * along)).astype(jnp.bfloat16)


def gradients(units, proto_s, proto_unit, col_inverse, exp_s, exp_t, scales, row_span):
    rows = units.shape[0]
    depth, share = proto_s.shape
    tile = math.gcd(rows, 8 * row_span)
    return pl.pallas_call(
        gradient_kernel,
        grid=(rows // tile,),
        out_shape=[
            jax.ShapeDtypeStruct((rows, depth), jnp.float32),
            jax.ShapeDtypeStruct((depth, share), jnp.bfloat16),
        ],
        in_specs=[
            pl.BlockSpec((tile, depth), lambda i: (i, 0)),
            pl.BlockSpec((depth, share), lambda i: (0, 0)),
            pl.BlockSpec((depth, share), lambda i: (0, 0)),
            pl.BlockSpec((1, share), lambda i: (0, 0)),
            pl.BlockSpec((tile, share), lambda i: (i, 0)),
            pl.BlockSpec((tile, share), lambda i: (i, 0)),
            pl.BlockSpec((tile, 2), lambda i: (i, 0)),
        ],
        out_specs=[
            pl.BlockSpec((tile, depth), lambda i: (i, 0)),
            pl.BlockSpec((depth, share), lambda i: (0, 0)),
        ],
        scratch_shapes=[pltpu.VMEM((depth, share), jnp.float32)],
        compiler_params=pltpu.CompilerParams(vmem_limit_bytes=48 * 2**20),
    )(units, proto_s, proto_unit, col_inverse, exp_s, exp_t, scales)


def shards(
    student_cls,
    student_patches,
    teacher_cls,
    teacher_patches,
    mask_index,
    crop_pair,
    center,
    student_w1,
    student_w2,
    teacher_w1,
    teacher_w2,
    student_proto,
    teacher_proto,
):
    row_span = mask_index.shape[1] + 1
    masked_count = mask_index.shape[1]
    local_crops = student_cls.shape[0]
    proto_ways = lax.axis_size("proto")
    data_ways = lax.axis_size("dp")
    data_index = lax.axis_index("dp")
    crop_group = local_crops * proto_ways
    own_rows = local_crops * row_span
    group_rows = crop_group * row_span
    all_rows = group_rows * data_ways
    crops_total = crop_group * data_ways
    width = student_cls.shape[1]
    bottleneck = student_w2.shape[1]
    hidden_block = student_w1.shape[1]
    share = student_proto.shape[1] // data_ways

    rows_student = select_rows(student_cls, student_patches, mask_index)
    rows_teacher = select_rows(teacher_cls, teacher_patches, mask_index)
    pair_tile = jnp.broadcast_to(crop_pair[:, None, None], (local_crops, 8, 128))
    student_all, teacher_all, pairs, first_s, first_t = exchange(
        0,
        (rows_student, PROTO, True),
        (rows_teacher, PROTO, True),
        (pair_tile, PROTO, True),
        (student_w1, DATA, True),
        (teacher_w1, DATA, True),
    )
    student_all = student_all.reshape(group_rows, width)
    teacher_all = teacher_all.reshape(group_rows, width)
    pairs = pairs[:, :, 0, 0].reshape(crop_group)

    preact = jnp.dot(
        student_all, first_s.reshape(width, hidden_block), preferred_element_type=jnp.float32
    )
    hidden = jax.nn.gelu(preact, approximate=False).astype(jnp.bfloat16)
    part_s = jnp.dot(hidden, student_w2, preferred_element_type=jnp.float32)
    teacher_pre = jnp.dot(
        teacher_all, first_t.reshape(width, hidden_block), preferred_element_type=jnp.float32
    )
    teacher_hidden = jax.nn.gelu(teacher_pre, approximate=False).astype(jnp.bfloat16)
    part_t = jnp.dot(teacher_hidden, teacher_w2, preferred_element_type=jnp.float32)
    by_crop = part_t.reshape(crop_group, row_span, bottleneck)
    by_crop = jnp.concatenate([by_crop[:, 0][pairs][:, None], by_crop[:, 1:]], axis=1)
    parts_s, parts_t = exchange(
        1,
        (part_s.reshape(proto_ways, own_rows, bottleneck), PROTO, False),
        (
            by_crop.astype(jnp.bfloat16).reshape(proto_ways, own_rows, bottleneck),
            PROTO,
            False,
        ),
    )
    unit_s, inverse_s = normalize_rows(jnp.sum(parts_s, axis=0))
    unit_t, _ = normalize_rows(jnp.sum(parts_t.astype(jnp.float32), axis=0))
    packed = jnp.concatenate([unit_s, unit_t], axis=1).astype(jnp.bfloat16)
    (all_units,) = exchange(2, (packed, PROTO + DATA, True))
    all_units = all_units.reshape(all_rows, 2 * bottleneck)

    own_s = lax.dynamic_slice_in_dim(student_proto, data_index * share, share, axis=1)
    own_t = lax.dynamic_slice_in_dim(teacher_proto, data_index * share, share, axis=1)
    own_center = lax.dynamic_slice_in_dim(center, data_index * share, share, axis=1)
    proto_unit, col_inverse = normalize_columns(own_s)
    teacher_unit, _ = normalize_columns(own_t)
    proto_s_b = proto_unit.astype(jnp.bfloat16)
    proto_t_b = teacher_unit.astype(jnp.bfloat16)
    is_cls = jnp.arange(all_rows, dtype=jnp.int32) % row_span == 0
    exp_s, exp_t, sums = scores(all_units, proto_s_b, proto_t_b, own_center, row_span)
    sums = sums[:, :3].T
    (sums,) = exchange(3, (sums.reshape(-1, 128), PROTO + DATA, True))
    total_t, total_s, cross = jnp.sum(sums, axis=0).reshape(3, all_rows)
    weights = jnp.where(is_cls, 1.0 / crops_total, 1.0 / (crops_total * masked_count)).astype(
        jnp.float32
    )
    weighted_loss = weights * (jnp.log(total_s) - cross / total_t)
    loss_value = (
        jnp.sum(lax.dynamic_slice_in_dim(weighted_loss, data_index * group_rows, group_rows))
        * data_ways
    ).reshape(1)
    factor = loss_scale / student_temp * weights
    scales = jnp.stack([factor / total_s, factor / total_t], axis=1)
    grad_units, projected = gradients(
        all_units, proto_s_b, proto_unit, col_inverse, exp_s, exp_t, scales, row_span
    )
    (grad_units,) = exchange(
        4, (grad_units.reshape(data_ways, group_rows, bottleneck), DATA, False)
    )
    grad_units = jnp.sum(grad_units, axis=0).reshape(proto_ways, own_rows, bottleneck)
    projected = projected.reshape(
        data_ways, bottleneck // data_ways, share
    )
    half = bottleneck // data_ways // 2
    grad_units, upper = exchange(
        5, (grad_units, PROTO, False), (projected[:, :half], DATA, False)
    )
    grad_units = jnp.sum(grad_units, axis=0)
    grad_z = (
        inverse_s * (grad_units - unit_s * jnp.sum(unit_s * grad_units, axis=1, keepdims=True))
    ).astype(jnp.bfloat16)
    grad_z, lower = exchange(6, (grad_z, PROTO, True), (projected[:, half:], DATA, False))
    grad_proto = (
        jnp.concatenate([upper, lower], axis=1)
        .transpose(1, 0, 2)
        .reshape(2 * half, data_ways * share)
        .astype(jnp.float32)
    )
    grad_z = grad_z.reshape(group_rows, bottleneck)

    grad_hidden = lax.dot_general(
        grad_z, student_w2, (((1,), (1,)), ((), ())), preferred_element_type=jnp.float32
    )
    grad_pre = (grad_hidden * gelu_grad(preact)).astype(jnp.bfloat16)
    part_w1 = contract_rows(student_all, grad_pre).astype(jnp.bfloat16)
    part_w2 = contract_rows(hidden, grad_z).astype(jnp.bfloat16)
    part_w1, part_w2 = exchange(
        7,
        (part_w1.reshape(data_ways, width // data_ways, hidden_block), DATA, False),
        (part_w2, DATA, True),
    )
    grad_w1 = jnp.sum(part_w1.astype(jnp.float32), axis=0)
    grad_w2 = jnp.sum(part_w2.astype(jnp.float32), axis=0)
    return (loss_value, grad_w1, grad_w2, grad_proto)


def solution(mesh):
    placed = (
        P(("dp", "proto"), None),
        P(("dp", "proto"), None, None),
        P(("dp", "proto"), None),
        P(("dp", "proto"), None, None),
        P(("dp", "proto"), None),
        P(("dp", "proto")),
        P(None, "proto"),
        P("dp", "proto"),
        P("proto", None),
        P("dp", "proto"),
        P("proto", None),
        P(None, "proto"),
        P(None, "proto"),
    )
    return jax.shard_map(
        shards,
        mesh=mesh,
        in_specs=placed,
        out_specs=(P("dp"), P("dp", "proto"), P("proto", None), P("dp", "proto")),
        check_vma=False,
    )
```
